32 devices in a mesh: dom: 2 (over x), term: 8 (over z, y), doc: 2 (over core).
Axes of the slice: x: 2, y: 2, z: 4, core: 2. Of those that a mesh axis runs over, the one named last changes fastest.
Arguments:
- w_rows: bfloat16 [8192, 128], P(('dom', 'term', 'doc')), parts along dimension 0
- h_cols: bfloat16 [128, 262144], P(None, ('dom', 'term', 'doc')), parts along dimension 1, may hold values from 0.19921875 to 2
- blocks: bfloat16 [16, 2, 64, 256, 256], P(('dom', 'term'), 'doc'), parts along dimension 0, may hold values from 2992 to 29952
- block_row: int32 [16, 2, 64], P(('dom', 'term'), 'doc'), parts along dimension 0, may hold values from 0 to 7
- block_col: int32 [16, 2, 64], P(('dom', 'term'), 'doc'), parts along dimension 0, may hold values from 0 to 63
- block_count: int32 [16, 2], P(('dom', 'term'), 'doc'), parts along dimension 0, may hold values from 8 to 64, as said below
Outputs:
- w_next: bfloat16 [8192, 128], P(('dom', 'term', 'doc')), parts along dimension 0
- h_next: bfloat16 [128, 262144], P(None, ('dom', 'term', 'doc')), parts along dimension 1
The draws below stay inside these ranges and needn't reach their ends.
There are 2 independent parts, one for each index of `dom`. The reference program is written for one: setup_inputs(seed, part) draws one part's arguments, and reference() takes and returns one part's arrays. A program takes and returns all parts, laid end to end along the dimension named above; each array names one. Nothing has to cross between parts.
Inputs may be any that keep to these rules, and one draw needn't show every extreme that they name: `block_count`: some tile has exactly 64 live slots in every draw; slots at or beyond a tile's count hold values that are not part of X.
All inputs are finite; a program needn't handle non-finite values.
Results may differ from the reference program's by a relative error of at most 0.0026.
Values may be sent and summed in bfloat16 or wider, within the bound.
A program may use at most 128 MiB of HBM per device.

```python
import math
import jax
import jax.numpy as jnp
from jax import lax

K = 128
BS = 256
TERM_DEV = 8192
DOC_DEV = 256
NB = 64
TERMS = 131072
N_TERM = 8
N_DOC = 2


def draw_w_rows(key, part):
    key = jax.random.fold_in(key, 11)
    key_rows, key_cols, key_noise = jax.random.split(key, 3)
    total = DOC_DEV * N_TERM * N_DOC
    rising = 1.0 + 2.0 * jnp.arange(total, dtype=jnp.float32) / total
    row_scale = jnp.exp(jax.random.uniform(key_rows, (total, 1), jnp.float32, 0.0, jnp.log(10.0)))
    col_scale = jnp.exp(jax.random.uniform(key_cols, (1, K), jnp.float32, 0.0, jnp.log(10.0)))
    noise = jnp.exp(jax.random.uniform(key_noise, (total, K), jnp.float32, jnp.log(0.5), jnp.log(2.0)))
    return (0.05 * rising[:, None] * row_scale * col_scale * noise).astype(jnp.bfloat16)


def draw_block_count(key, part):
    key = jax.random.fold_in(key, 5)
    key_level, key_pick = jax.random.split(key)
    tile_count = N_TERM * N_DOC
    level = jax.random.randint(key_level, (tile_count,), 0, 4)
    counts = jnp.where(level == 0, NB, jnp.where(level == 3, NB // 8, NB // 4))
    chosen = jax.random.randint(key_pick, (), 0, tile_count)
    counts = jnp.where(jnp.arange(tile_count) == chosen, NB, counts)
    return counts.reshape(N_TERM, N_DOC).astype(jnp.int32)


def touch_ends(drawn, key, smallest, top_value):
    extent = drawn.shape
    index_at = [jax.random.randint(jax.random.fold_in(key, axis), (), 0, extent[axis]) for axis in range(len(extent))]
    drawn = drawn.at[tuple(index_at)].set(smallest)
    longest = extent.index(max(extent))
    index_at[longest] = (index_at[longest] + 1) % extent[longest]
    return drawn.at[tuple(index_at)].set(top_value)


def block_scale(stream_key, extent, shards, least, top_value):
    loudness = 1.0
    for dim, shards_of in shards:
        steps = jax.random.uniform(jax.random.fold_in(jax.random.fold_in(stream_key, 6), dim), (shards_of,), jnp.float32, least / len(shards), top_value / len(shards))
        loudness = loudness * jnp.repeat(jnp.exp(steps), extent[dim] // shards_of).reshape((-1,) + (1,) * (len(extent) - 1 - dim))
    return loudness


def setup_inputs(seed: int = 0, part: int = 0) -> dict:
    splits = jax.random.split(jax.random.key(seed), 7)
    part_splits = jax.random.split(jax.random.fold_in(splits[6], part), 7)
    return {
        "w_rows": draw_w_rows(jax.random.fold_in(jax.random.fold_in(splits[6], part), 71), part),
        "h_cols": jnp.clip(jnp.exp(math.log(2.0) - 2.306499 * jax.random.uniform(part_splits[1], (K, TERMS), jnp.float32) ** block_scale(part_splits[1], (K, TERMS), ((1, 16),), -0.2, 0.2)), 0.19921875, 2.0).astype(jnp.bfloat16),
        "blocks": jnp.clip(jnp.exp(math.log(29952.0) - 2.303654 * jax.random.uniform(part_splits[2], (N_TERM, N_DOC, NB, BS, BS), jnp.float32) ** block_scale(part_splits[2], (N_TERM, N_DOC, NB, BS, BS), ((0, 8), (1, 2)), -0.2, 0.2)), 2992.0, 29952.0).astype(jnp.bfloat16),
        "block_row": touch_ends(jax.random.randint(part_splits[3], (N_TERM, N_DOC, NB), 0, N_TERM * DOC_DEV // BS), jax.random.fold_in(part_splits[3], 1), 0, (N_TERM * DOC_DEV // BS) - 1).astype(jnp.int32),
        "block_col": touch_ends(jax.random.randint(part_splits[4], (N_TERM, N_DOC, NB), 0, N_DOC * TERM_DEV // BS), jax.random.fold_in(part_splits[4], 1), 0, (N_DOC * TERM_DEV // BS) - 1).astype(jnp.int32),
        "block_count": draw_block_count(jax.random.fold_in(jax.random.fold_in(splits[6], part), 71), part),
    }


def tile_parts(w_part, h_tiles, blocks, block_row, block_col, block_count, k_dim):
    grid_rows = N_TERM * DOC_DEV // BS
    grid_cols = N_DOC * TERM_DEV // BS
    col_ids = jnp.arange(grid_cols, dtype=jnp.int32)
    slot_ids = jnp.arange(NB, dtype=jnp.int32)

    def one_tile(index):
        term_idx = index // N_DOC
        doc_idx = index % N_DOC
        doc_group = w_part[:, doc_idx].reshape(grid_rows, BS, k_dim)
        tile_values = blocks[term_idx, doc_idx].astype(jnp.float32)
        slot_rows = block_row[term_idx, doc_idx]
        slot_cols = block_col[term_idx, doc_idx]
        live_slots = slot_ids < block_count[term_idx, doc_idx]
        picked = jnp.take(doc_group, slot_rows, axis=0).astype(jnp.float32)
        products = jnp.einsum("sbk,sbc->skc", picked, tile_values)
        col_hits = jnp.where(live_slots[:, None], slot_cols[:, None] == col_ids[None, :], False).astype(jnp.float32)
        numer_tile = jnp.einsum("skc,sj->kjc", products, col_hits, precision=lax.Precision.HIGHEST)
        return numer_tile.reshape(k_dim, grid_cols * BS)

    return one_tile


def reference(w_rows, h_cols, blocks, block_row, block_col, block_count):
    k_dim = w_rows.shape[1]
    grid_rows = N_TERM * DOC_DEV // BS
    grid_cols = N_DOC * TERM_DEV // BS
    w_by_doc = w_rows.reshape(N_TERM, N_DOC, DOC_DEV, k_dim)
    w_stack = jnp.transpose(w_by_doc, (0, 2, 1, 3)).reshape(N_TERM * DOC_DEV, N_DOC, k_dim)
    tile_count = N_TERM * N_DOC
    indices = jnp.arange(tile_count, dtype=jnp.int32)
    one_tile = tile_parts(w_stack, None, blocks, block_row, block_col, block_count, k_dim)
    numer_tiles = lax.map(one_tile, indices).reshape(N_TERM, N_DOC, k_dim, grid_cols * BS)
    numer_h = jnp.sum(numer_tiles, axis=1)
    numer_h = jnp.transpose(numer_h, (1, 0, 2)).reshape(k_dim, N_TERM * grid_cols * BS)
    gram_w = jnp.dot(w_rows.T, w_rows, preferred_element_type=jnp.float32)
    h_float = h_cols.astype(jnp.float32)
    h_next = (h_float * numer_h / jnp.dot(gram_w, h_float, precision=lax.Precision.HIGHEST)).astype(jnp.bfloat16)
    h_tiles = h_next.reshape(k_dim, N_TERM, grid_cols, BS)
    gram_h = jnp.dot(h_next, h_next.T, preferred_element_type=jnp.float32)
    row_ids = jnp.arange(grid_rows, dtype=jnp.int32)
    slot_ids = jnp.arange(NB, dtype=jnp.int32)

    def row_tile(index):
        term_idx = index // N_DOC
        doc_idx = index % N_DOC
        tile_values = blocks[term_idx, doc_idx].astype(jnp.float32)
        slot_rows = block_row[term_idx, doc_idx]
        slot_cols = block_col[term_idx, doc_idx]
        live_slots = slot_ids < block_count[term_idx, doc_idx]
        term_tile = h_tiles[:, term_idx]
        chosen = jnp.take(term_tile, slot_cols, axis=1).astype(jnp.float32)
        backward = jnp.einsum("sbc,ksc->sbk", tile_values, chosen)
        row_hits = jnp.where(live_slots[:, None], slot_rows[:, None] == row_ids[None, :], False).astype(jnp.float32)
        part_rows = jnp.einsum("sbk,sr->rbk", backward, row_hits, precision=lax.Precision.HIGHEST)
        return part_rows.reshape(grid_rows * BS, k_dim)

    row_terms = lax.map(row_tile, indices).reshape(N_TERM, N_DOC, N_TERM * DOC_DEV, k_dim)
    numer_w = jnp.sum(row_terms, axis=0).reshape(N_DOC, N_TERM, DOC_DEV, k_dim)
    numer_w = jnp.transpose(numer_w, (1, 0, 2, 3)).reshape(N_TERM * N_DOC * DOC_DEV, k_dim)
    w_float = w_rows.astype(jnp.float32)
    w_next = (w_float * numer_w / jnp.dot(w_float, gram_h, precision=lax.Precision.HIGHEST)).astype(jnp.bfloat16)
    return w_next, h_next
```

```python
import functools

import jax
import jax.numpy as jnp
from jax import lax
from jax.experimental import pallas as pl
from jax.experimental.pallas import tpu as pltpu
from jax.sharding import PartitionSpec as P

MESH = pl.DeviceIdType.MESH
F32 = jnp.float32
BF16 = jnp.bfloat16
CHUNKS = 4
LOADS = 8


def dot(a, b):
    return jnp.dot(a, b, preferred_element_type=F32)


def dot_nt(a, b):
    return lax.dot_general(a, b, (((1,), (1,)), ((), ())), preferred_element_type=F32)


def three_parts(a):
    top = a.astype(BF16)
    rest = a - top.astype(F32)
    middle = rest.astype(BF16)
    return top, middle, (rest - middle.astype(F32)).astype(BF16)


def kernel(
    n, slots, own, width,
    links, w_ref, h_hbm, x_hbm,
    w_out, h_out,
    x, h_in, wt, prod, back, num_out, num_in, h_all, gw, gw_in, gw_parts,
    gh, gh_in, gh_all, gh_full, rs_out, rs_in,
    load_sem, hin_sem, wsend, wrecv, gwsem, nsend, nrecv, hsend, hrecv, hout_sem,
    ghsem, gasend, garecv, rsend, rrecv,
):
    me = lax.axis_index("term")
    doc = lax.axis_index("doc")
    other = 1 - doc
    k = w_ref.shape[1]
    per = own // CHUNKS
    load_size = slots // LOADS
    half = k // 2
    grid_cols = 2 * own

    def load(i):
        part = pl.ds(i * load_size, load_size)
        return pltpu.make_async_copy(x_hbm.at[part], x.at[part], load_sem.at[i])

    for i in range(LOADS):
        load(i).start()
    h_load = pltpu.make_async_copy(h_hbm, h_in, hin_sem)
    h_load.start()

    barrier = pltpu.get_barrier_semaphore()

    def greet(o, _):
        pl.semaphore_signal(barrier, inc=1, device_id={"term": lax.rem(me + o, n)}, device_id_type=MESH)
        return 0

    pl.semaphore_signal(barrier, inc=1, device_id={"doc": other}, device_id_type=MESH)
    lax.fori_loop(1, n, greet, 0)
    wt[me] = w_ref[...].astype(F32).T.astype(BF16)
    pl.semaphore_wait(barrier, n)

    def to_peer(src, dst, send, recv, target):
        return pltpu.make_async_remote_copy(
            src_ref=src, dst_ref=dst, send_sem=send, recv_sem=recv,
            device_id={"term": target}, device_id_type=MESH,
        )

    def to_partner(src, dst, send, recv):
        return pltpu.make_async_remote_copy(
            src_ref=src, dst_ref=dst, send_sem=send, recv_sem=recv,
            device_id={"doc": other}, device_id_type=MESH,
        )

    def w_copy(slot, target):
        return to_peer(wt.at[slot], wt.at[slot], wsend.at[target], wrecv.at[slot], target)

    def send_w(o, _):
        w_copy(me, lax.rem(me + o, n)).start()
        return 0

    lax.fori_loop(1, n, send_w, 0)
    prod[slots] = jnp.zeros_like(prod[slots])
    back[slots] = jnp.zeros_like(back[slots])
    gw[...] = dot_nt(wt[me], wt[me])

    def take_w(o, _):
        source = lax.rem(me + n - o, n)
        w_copy(source, source).wait_recv()
        gw[...] += dot_nt(wt[source], wt[source])
        return 0

    lax.fori_loop(1, n, take_w, 0)
    gw_copy = to_partner(gw, gw_in, gwsem.at[0], gwsem.at[1])
    gw_copy.start()

    for i in range(LOADS):
        load(i).wait()

        def forward(s, _):
            term = dot(wt[links[2, s]], x[s])
            prod[s] = prod[links[0, s]] + term
            return 0

        lax.fori_loop(i * load_size, (i + 1) * load_size, forward, 0, unroll=2)

    def num_copy(i):
        part = pl.ds(i * per, per)
        return to_partner(num_out.at[part], num_in.at[part], nsend.at[i], nrecv.at[i])

    for i in range(CHUNKS):

        def stage(j, _):
            num_out[j] = prod[links[4, other * own + j]]
            return 0

        lax.fori_loop(i * per, (i + 1) * per, stage, 0)
        num_copy(i).start()

    gw_copy.wait()
    top, middle, low = three_parts(gw[...] + gw_in[...])
    gw_parts[0] = top
    gw_parts[1] = middle
    gw_parts[2] = low
    gh[...] = jnp.zeros_like(gh)
    h_load.wait()

    def h_copy(i):
        part = pl.ds(doc * own + i * per, per)
        return to_partner(h_all.at[part], h_all.at[part], hsend.at[i], hrecv.at[i])

    def h_take(i):
        part = pl.ds(other * own + i * per, per)
        return to_partner(h_all.at[part], h_all.at[part], hsend.at[i], hrecv.at[i])

    def h_store(j):
        cols = pl.ds(pl.multiple_of(j * width, width), width)
        return pltpu.make_async_copy(h_all.at[doc * own + j], h_out.at[:, cols], hout_sem.at[j])

    for i in range(CHUNKS):
        num_copy(i).wait()

        def update(j, _):
            cols = pl.ds(pl.multiple_of(j * width, width), width)
            old = h_in[:, cols]
            denominator = dot(gw_parts[0], old) + (dot(gw_parts[1], old) + dot(gw_parts[2], old))
            numerator = prod[links[4, doc * own + j]] + num_in[j]
            new = (old.astype(F32) * numerator / denominator).astype(BF16)
            h_all[doc * own + j] = new
            gh[...] += dot_nt(new, new)
            h_store(j).start()
            return 0

        lax.fori_loop(i * per, (i + 1) * per, update, 0)
        h_copy(i).start()

    my_half = pl.ds(pl.multiple_of(doc * half, half), half)
    its_half = pl.ds(pl.multiple_of(other * half, half), half)
    gh_copy = to_partner(gh.at[its_half], gh_in, ghsem.at[0], ghsem.at[1])
    gh_copy.start()
    gh_copy.wait()
    gh_all[me] = gh[my_half] + gh_in[...]

    def ga_copy(slot, target):
        return to_peer(gh_all.at[slot], gh_all.at[slot], gasend.at[target], garecv.at[slot], target)

    def send_ga(o, _):
        ga_copy(me, lax.rem(me + o, n)).start()
        return 0

    lax.fori_loop(1, n, send_ga, 0)
    for i in range(CHUNKS):
        h_take(i).wait_recv()

    def backward(s, _):
        term = dot_nt(x[s], h_all[links[3, s]])
        back[s] = back[links[1, s]] + term
        return 0

    lax.fori_loop(0, slots, backward, 0, unroll=2)

    def rs_copy(target):
        return to_peer(rs_out.at[target], rs_in.at[me], rsend.at[target], rrecv.at[me], target)

    def rs_take(source):
        return to_peer(rs_out.at[source], rs_in.at[source], rsend.at[source], rrecv.at[source], source)

    def send_rows(o, _):
        target = lax.rem(me + o, n)
        rs_out[target] = back[links[5, target]]
        rs_copy(target).start()
        return 0

    lax.fori_loop(1, n, send_rows, 0)

    def take_ga(o, total):
        source = lax.rem(me + n - o, n)
        ga_copy(source, source).wait_recv()
        return total + gh_all[source]

    gh_full[my_half] = lax.fori_loop(1, n, take_ga, gh_all[me])
    full_copy = to_partner(gh_full.at[my_half], gh_full.at[my_half], ghsem.at[2], ghsem.at[3])
    full_copy.start()
    full_take = to_partner(gh_full.at[its_half], gh_full.at[its_half], ghsem.at[2], ghsem.at[3])
    full_take.wait_recv()
    top, middle, low = three_parts(gh_full[...])
    w = w_ref[...]
    denominator = dot(w, top) + (dot(w, middle) + dot(w, low))

    def take_rows(o, total):
        source = lax.rem(me + n - o, n)
        rs_take(source).wait_recv()
        return total + rs_in[source]

    numerator = lax.fori_loop(1, n, take_rows, back[links[5, me]])
    w_out[...] = (w.astype(F32) * numerator / denominator).astype(BF16)

    def settle(o, _):
        target = lax.rem(me + o, n)
        w_copy(me, target).wait_send()
        ga_copy(me, target).wait_send()
        rs_copy(target).wait_send()
        return 0

    lax.fori_loop(1, n, settle, 0)
    full_copy.wait_send()
    for i in range(CHUNKS):
        h_copy(i).wait_send()

    def stored(j, _):
        h_store(j).wait()
        return 0

    lax.fori_loop(0, own, stored, 0)


def local(n, w_rows, h_cols, blocks, block_row, block_col, block_count):
    k = w_rows.shape[1]
    slots, width = blocks.shape[2], blocks.shape[3]
    own_cols = h_cols.shape[1]
    own = own_cols // width
    grid_cols = 2 * own
    rows, cols, count = block_row[0, 0], block_col[0, 0], block_count[0, 0]
    span = max(slots, grid_cols, n)
    slot_ids = jnp.arange(slots, dtype=jnp.int32)
    ids = jnp.arange(span, dtype=jnp.int32)
    pad = lambda a: jnp.pad(a, (0, span - slots))

    def latest(keys, wanted, limit):
        hit = (keys[None, :] == wanted[:, None]) & (slot_ids[None, :] < jnp.minimum(limit, count)[:, None])
        found = jnp.max(jnp.where(hit, slot_ids[None, :], -1), axis=1)
        return jnp.where(found < 0, slots, found)

    full = jnp.full((span,), slots, jnp.int32)
    links = jnp.stack([
        latest(cols, pad(cols), ids),
        latest(rows, pad(rows), ids),
        pad(rows),
        pad(cols),
        latest(cols, ids, full),
        latest(rows, ids, full),
    ])
    dma = pltpu.SemaphoreType.DMA
    return pl.pallas_call(
        functools.partial(kernel, n, slots, own, width),
        out_shape=(
            jax.ShapeDtypeStruct(w_rows.shape, BF16),
            jax.ShapeDtypeStruct(h_cols.shape, BF16),
        ),
        in_specs=[
            pl.BlockSpec(memory_space=pltpu.SMEM),
            pl.BlockSpec(memory_space=pltpu.VMEM),
            pl.BlockSpec(memory_space=pl.ANY),
            pl.BlockSpec(memory_space=pl.ANY),
        ],
        out_specs=(pl.BlockSpec(memory_space=pltpu.VMEM), pl.BlockSpec(memory_space=pl.ANY)),
        scratch_shapes=[
            pltpu.VMEM((slots, width, width), BF16),
            pltpu.VMEM((k, own_cols), BF16),
            pltpu.VMEM((n, k, width), BF16),
            pltpu.VMEM((slots + 1, k, width), F32),
            pltpu.VMEM((slots + 1, width, k), F32),
            pltpu.VMEM((own, k, width), F32),
            pltpu.VMEM((own, k, width), F32),
            pltpu.VMEM((grid_cols, k, width), BF16),
            pltpu.VMEM((k, k), F32),
            pltpu.VMEM((k, k), F32),
            pltpu.VMEM((3, k, k), BF16),
            pltpu.VMEM((k, k), F32),
            pltpu.VMEM((k // 2, k), F32),
            pltpu.VMEM((n, k // 2, k), F32),
            pltpu.VMEM((k, k), F32),
            pltpu.VMEM((n, width, k), F32),
            pltpu.VMEM((n, width, k), F32),
            dma((LOADS,)),
            dma,
            dma((n,)),
            dma((n,)),
            dma((2,)),
            dma((CHUNKS,)),
            dma((CHUNKS,)),
            dma((CHUNKS,)),
            dma((CHUNKS,)),
            dma((own,)),
            dma((4,)),
            dma((n,)),
            dma((n,)),
            dma((n,)),
            dma((n,)),
        ],
        compiler_params=pltpu.CompilerParams(
            collective_id=0, has_side_effects=True, vmem_limit_bytes=58 * 1024 * 1024
        ),
        cost_estimate=pl.CostEstimate(flops=4 * slots * width * width * k, bytes_accessed=2 * slots * width * width, transcendentals=0),
    )(links, w_rows, h_cols, blocks[0, 0])


def solution(mesh):
    placed = (
        P(("dom", "term", "doc"), None),
        P(None, ("dom", "term", "doc")),
        P(("dom", "term"), "doc", None, None, None),
        P(("dom", "term"), "doc", None),
        P(("dom", "term"), "doc", None),
        P(("dom", "term"), "doc"),
    )
    return jax.shard_map(
        functools.partial(local, mesh.shape["term"]),
        mesh=mesh,
        in_specs=placed,
        out_specs=(P(("dom", "term", "doc"), None), P(None, ("dom", "term", "doc"))),
        check_vma=False,
    )
```

```python
import functools

import jax
import jax.numpy as jnp
from jax import lax
from jax.experimental import pallas as pl
from jax.experimental.pallas import tpu as pltpu
from jax.sharding import PartitionSpec as P

MESH = pl.DeviceIdType.MESH
F32 = jnp.float32
BF16 = jnp.bfloat16
CHUNKS = 4
LOADS = 8
GROUP = 4
SCALE_ROWS = 16
NUMERATOR_SCALE = 65536.0


def dot(a, b):
    return jnp.dot(a, b, preferred_element_type=F32)


def dot_nt(a, b):
    return lax.dot_general(a, b, (((1,), (1,)), ((), ())), preferred_element_type=F32)


def two_parts(a):
    top = a.astype(BF16)
    return top, (a - top.astype(F32)).astype(BF16)


def power(v, squarings):
    size = v
    for _ in range(squarings):
        size = size * size
    return jnp.where(v < 0, -size, size).astype(BF16)


def root(code, squarings):
    code = code.astype(F32)
    size = jnp.abs(code)
    for _ in range(squarings):
        size = jnp.sqrt(size)
    return jnp.where(code < 0, -size, size)


def pack(ref, slot, value):
    rows = value.shape[0]
    top = jnp.max(jnp.abs(value), axis=0, keepdims=True)
    scale = jnp.maximum(top, 1e-30).astype(BF16).astype(F32)
    ref[slot, :rows] = power(value * (1.0 / scale), 3)
    ref[slot, rows:] = jnp.broadcast_to(scale, (SCALE_ROWS, value.shape[1])).astype(BF16)


def unpack(ref, slot, rows):
    scale = ref[slot, rows:].astype(F32)[:1]
    return root(ref[slot, :rows], 3) * scale


def norms(gram):
    k = gram.shape[0]
    row = lax.broadcasted_iota(jnp.int32, (k, k), 0)
    col = lax.broadcasted_iota(jnp.int32, (k, k), 1)
    square = jnp.sum(jnp.where(row == col, gram, 0.0), axis=1, keepdims=True)
    return jnp.maximum(jnp.sqrt(square), 1e-30) * NUMERATOR_SCALE


def kernel(
    n, slots, own, width,
    links, w_ref, h_hbm, x_hbm,
    w_out, h_out,
    x, h_in, wt, prod, back, num_out, num_in, h_all, gw, gw_in, gw_parts,
    gh, gh_in, gh_pair, gh_all, gh_full, y_out, y_in, z_out, z_in,
    load_sem, hin_sem, wsend, wpass, wrecv, gwsem, nsend, nrecv, hsend, hrecv, hout_sem,
    ghsem, gasend, garecv, ysend, yrecv, zsend, zrecv,
):
    me = lax.axis_index("term")
    doc = lax.axis_index("doc")
    other = 1 - doc
    pairs = n // 2
    side, place = lax.rem(me, 2), lax.div(me, 2)
    mate = me + 1 - 2 * side
    k = w_ref.shape[1]
    per = own // CHUNKS
    load_size = slots // LOADS
    half = k // 2

    def load(i):
        part = pl.ds(i * load_size, load_size)
        return pltpu.make_async_copy(x_hbm.at[part], x.at[part], load_sem.at[i])

    def line(o):
        return lax.rem(place + o, pairs)

    def to_term(src, dst, send, recv, target):
        return pltpu.make_async_remote_copy(
            src_ref=src, dst_ref=dst, send_sem=send, recv_sem=recv,
            device_id={"term": target}, device_id_type=MESH,
        )

    def to_core(src, dst, send, recv):
        return pltpu.make_async_remote_copy(
            src_ref=src, dst_ref=dst, send_sem=send, recv_sem=recv,
            device_id={"doc": other}, device_id_type=MESH,
        )

    barrier = pltpu.get_barrier_semaphore()
    pl.semaphore_signal(barrier, inc=1, device_id={"doc": other}, device_id_type=MESH)
    pl.semaphore_signal(barrier, inc=1, device_id={"term": mate}, device_id_type=MESH)

    def greet(o, _):
        pl.semaphore_signal(barrier, inc=1, device_id={"term": 2 * line(o) + side}, device_id_type=MESH)
        return 0

    lax.fori_loop(1, pairs, greet, 0)
    for i in range(LOADS):
        load(i).start()
    h_load = pltpu.make_async_copy(h_hbm, h_in, hin_sem)
    h_load.start()
    wt[me] = w_ref[...].astype(F32).T.astype(BF16)
    pl.semaphore_wait(barrier, pairs + 1)

    def w_copy(slot, at):
        return to_term(wt.at[slot], wt.at[slot], wsend.at[at], wrecv.at[slot], 2 * at + side)

    def w_pass(slot):
        return to_term(wt.at[slot], wt.at[slot], wpass.at[lax.div(slot, 2)], wrecv.at[slot], mate)

    def send_w(o, _):
        w_copy(me, line(o)).start()
        return 0

    lax.fori_loop(1, pairs, send_w, 0)
    w_pass(me).start()
    prod[slots] = jnp.zeros_like(prod[slots])
    back[slots] = jnp.zeros_like(back[slots])
    gw[...] = dot_nt(wt[me], wt[me])

    def take_w(o, _):
        at = line(pairs - o)
        source = 2 * at + side
        w_copy(source, at).wait_recv()
        w_pass(source).start()
        gw[...] += dot_nt(wt[source], wt[source])
        return 0

    lax.fori_loop(1, pairs, take_w, 0)

    def take_passed(o, _):
        source = 2 * line(pairs - o) + 1 - side
        w_pass(source).wait_recv()
        gw[...] += dot_nt(wt[source], wt[source])
        return 0

    lax.fori_loop(0, pairs, take_passed, 0)
    gw_copy = to_core(gw, gw_in, gwsem.at[0], gwsem.at[1])
    gw_copy.start()

    for i in range(LOADS):
        load(i).wait()

        def forward(g, _):
            ids = [g * GROUP + t for t in range(GROUP)]
            terms = [dot(wt[links[2, s]], x[s]) for s in ids]
            for s, term in zip(ids, terms):
                prod[s] = prod[links[0, s]] + term
            return 0

        lax.fori_loop(i * load_size // GROUP, (i + 1) * load_size // GROUP, forward, 0)

    def num_copy(i):
        part = pl.ds(i * per, per)
        return to_core(num_out.at[part], num_in.at[part], nsend.at[i], nrecv.at[i])

    inverse = 1.0 / norms(gw[...])
    for i in range(CHUNKS):

        def stage(j, _):
            num_out[j] = power(prod[links[4, other * own + j]] * inverse, 2)
            return 0

        lax.fori_loop(i * per, (i + 1) * per, stage, 0)
        num_copy(i).start()

    gw_copy.wait()
    top, low = two_parts(gw[...] + gw_in[...])
    gw_parts[:, :k] = top
    gw_parts[:, k:] = low
    sent_scale = norms(gw_in[...])
    gh[...] = jnp.zeros_like(gh)
    h_load.wait()

    def h_copy(i):
        part = pl.ds(doc * own + i * per, per)
        return to_core(h_all.at[part], h_all.at[part], hsend.at[i], hrecv.at[i])

    def h_take(i):
        part = pl.ds(other * own + i * per, per)
        return to_core(h_all.at[part], h_all.at[part], hsend.at[i], hrecv.at[i])

    def h_store(j):
        cols = pl.ds(pl.multiple_of(j * width, width), width)
        return pltpu.make_async_copy(h_all.at[doc * own + j], h_out.at[:, cols], hout_sem.at[j])

    for i in range(CHUNKS):
        num_copy(i).wait()

        def update(g, _):
            news = []
            for j in (2 * g, 2 * g + 1):
                cols = pl.ds(pl.multiple_of(j * width, width), width)
                old = h_in[:, cols]
                denominator = dot(gw_parts[...], jnp.concatenate([old, old], axis=0))
                numerator = prod[links[4, doc * own + j]] + root(num_in[j], 2) * sent_scale
                new = (old.astype(F32) * numerator / denominator).astype(BF16)
                h_all[doc * own + j] = new
                news.append(new)
            gh[...] += dot_nt(news[0], news[0]) + dot_nt(news[1], news[1])
            for j in (2 * g, 2 * g + 1):
                h_store(j).start()
            return 0

        lax.fori_loop(i * per // 2, (i + 1) * per // 2, update, 0)
        h_copy(i).start()

    my_half = pl.ds(pl.multiple_of(doc * half, half), half)
    its_half = pl.ds(pl.multiple_of(other * half, half), half)
    gh_copy = to_core(gh.at[its_half], gh_in, ghsem.at[0], ghsem.at[1])
    gh_copy.start()
    gh_copy.wait()
    gh_pair[0] = gh[my_half] + gh_in[...]
    pair_copy = to_term(gh_pair.at[0], gh_pair.at[1], ghsem.at[2], ghsem.at[3], mate)
    pair_copy.start()
    for i in range(CHUNKS):
        h_take(i).wait_recv()
    pair_copy.wait()
    gh_all[place] = gh_pair[0] + gh_pair[1]

    def ga_copy(slot, at):
        return to_term(gh_all.at[slot], gh_all.at[slot], gasend.at[at], garecv.at[slot], 2 * at + side)

    def send_ga(o, _):
        ga_copy(place, line(o)).start()
        return 0

    lax.fori_loop(1, pairs, send_ga, 0)

    def backward(g, _):
        ids = [g * GROUP + t for t in range(GROUP)]
        terms = [dot_nt(x[s], h_all[links[3, s]]) for s in ids]
        for s, term in zip(ids, terms):
            back[s] = back[links[1, s]] + term
        return 0

    lax.fori_loop(0, slots // GROUP, backward, 0)

    def y_copy(at):
        return to_term(y_out.at[at], y_in.at[at], ysend.at[at], yrecv.at[at], mate)

    def z_copy(at):
        return to_term(z_out.at[at], z_in.at[place], zsend.at[at], zrecv.at[place], 2 * at + side)

    def z_take(at):
        return to_term(z_out.at[at], z_in.at[at], zsend.at[at], zrecv.at[at], 2 * at + side)

    def send_mate(o, _):
        at = line(o)
        pack(y_out, at, back[links[5, 2 * at + 1 - side]])
        y_copy(at).start()
        return 0

    lax.fori_loop(1, pairs + 1, send_mate, 0)

    def send_line(o, _):
        at = line(o)
        y_copy(at).wait_recv()
        pack(z_out, at, back[links[5, 2 * at + side]] + unpack(y_in, at, width))
        z_copy(at).start()
        return 0

    lax.fori_loop(1, pairs, send_line, 0)

    def take_ga(o, total):
        at = line(pairs - o)
        ga_copy(at, at).wait_recv()
        return total + gh_all[at]

    gh_full[my_half] = lax.fori_loop(1, pairs, take_ga, gh_all[place])
    full_copy = to_core(gh_full.at[my_half], gh_full.at[my_half], ghsem.at[4], ghsem.at[5])
    full_copy.start()
    y_copy(place).wait_recv()
    mine = back[links[5, me]] + unpack(y_in, place, width)
    full_take = to_core(gh_full.at[its_half], gh_full.at[its_half], ghsem.at[4], ghsem.at[5])
    full_take.wait_recv()
    top, low = two_parts(gh_full[...])
    w = w_ref[...]
    denominator = dot(w, top) + dot(w, low)

    def take_line(o, total):
        at = line(pairs - o)
        z_take(at).wait_recv()
        return total + unpack(z_in, at, width)

    numerator = lax.fori_loop(1, pairs, take_line, mine)
    w_out[...] = (w.astype(F32) * numerator / denominator).astype(BF16)

    def settle(o, _):
        at = line(o)
        w_copy(me, at).wait_send()
        ga_copy(place, at).wait_send()
        z_copy(at).wait_send()
        return 0

    lax.fori_loop(1, pairs, settle, 0)

    def settle_mate(at, _):
        w_pass(2 * at + side).wait_send()
        y_copy(at).wait_send()
        return 0

    lax.fori_loop(0, pairs, settle_mate, 0)
    full_copy.wait_send()
    for i in range(CHUNKS):
        h_copy(i).wait_send()

    def stored(j, _):
        h_store(j).wait()
        return 0

    lax.fori_loop(0, own, stored, 0)


def local(n, w_rows, h_cols, blocks, block_row, block_col, block_count):
    k = w_rows.shape[1]
    slots, width = blocks.shape[2], blocks.shape[3]
    own_cols = h_cols.shape[1]
    own = own_cols // width
    grid_cols = 2 * own
    rows, cols, count = block_row[0, 0], block_col[0, 0], block_count[0, 0]
    span = max(slots, grid_cols, n)
    slot_ids = jnp.arange(slots, dtype=jnp.int32)
    ids = jnp.arange(span, dtype=jnp.int32)
    pad = lambda a: jnp.pad(a, (0, span - slots))

    def latest(keys, wanted, limit):
        hit = (keys[None, :] == wanted[:, None]) & (slot_ids[None, :] < jnp.minimum(limit, count)[:, None])
        found = jnp.max(jnp.where(hit, slot_ids[None, :], -1), axis=1)
        return jnp.where(found < 0, slots, found)

    full = jnp.full((span,), slots, jnp.int32)
    links = jnp.stack([
        latest(cols, pad(cols), ids),
        latest(rows, pad(rows), ids),
        pad(rows),
        pad(cols),
        latest(cols, ids, full),
        latest(rows, ids, full),
    ])
    dma = pltpu.SemaphoreType.DMA
    return pl.pallas_call(
        functools.partial(kernel, n, slots, own, width),
        out_shape=(
            jax.ShapeDtypeStruct(w_rows.shape, BF16),
            jax.ShapeDtypeStruct(h_cols.shape, BF16),
        ),
        in_specs=[
            pl.BlockSpec(memory_space=pltpu.SMEM),
            pl.BlockSpec(memory_space=pltpu.VMEM),
            pl.BlockSpec(memory_space=pl.ANY),
            pl.BlockSpec(memory_space=pl.ANY),
        ],
        out_specs=(pl.BlockSpec(memory_space=pltpu.VMEM), pl.BlockSpec(memory_space=pl.ANY)),
        scratch_shapes=[
            pltpu.VMEM((slots, width, width), BF16),
            pltpu.VMEM((k, own_cols), BF16),
            pltpu.VMEM((n, k, width), BF16),
            pltpu.VMEM((slots + 1, k, width), F32),
            pltpu.VMEM((slots + 1, width, k), F32),
            pltpu.VMEM((own, k, width), BF16),
            pltpu.VMEM((own, k, width), BF16),
            pltpu.VMEM((grid_cols, k, width), BF16),
            pltpu.VMEM((k, k), F32),
            pltpu.VMEM((k, k), F32),
            pltpu.VMEM((k, 2 * k), BF16),
            pltpu.VMEM((k, k), F32),
            pltpu.VMEM((k // 2, k), F32),
            pltpu.VMEM((2, k // 2, k), F32),
            pltpu.VMEM((n // 2, k // 2, k), F32),
            pltpu.VMEM((k, k), F32),
            pltpu.VMEM((n // 2, width + SCALE_ROWS, k), BF16),
            pltpu.VMEM((n // 2, width + SCALE_ROWS, k), BF16),
            pltpu.VMEM((n // 2, width + SCALE_ROWS, k), BF16),
            pltpu.VMEM((n // 2, width + SCALE_ROWS, k), BF16),
            dma((LOADS,)),
            dma,
            dma((n // 2,)),
            dma((n // 2,)),
            dma((n,)),
            dma((2,)),
            dma((CHUNKS,)),
            dma((CHUNKS,)),
            dma((CHUNKS,)),
            dma((CHUNKS,)),
            dma((own,)),
            dma((6,)),
            dma((n // 2,)),
            dma((n // 2,)),
            dma((n // 2,)),
            dma((n // 2,)),
            dma((n // 2,)),
            dma((n // 2,)),
        ],
        compiler_params=pltpu.CompilerParams(
            collective_id=0, has_side_effects=True, vmem_limit_bytes=58 * 1024 * 1024
        ),
        cost_estimate=pl.CostEstimate(flops=4 * slots * width * width * k, bytes_accessed=2 * slots * width * width, transcendentals=0),
    )(links, w_rows, h_cols, blocks[0, 0])


def solution(mesh):
    placed = (
        P(("dom", "term", "doc"), None),
        P(None, ("dom", "term", "doc")),
        P(("dom", "term"), "doc", None, None, None),
        P(("dom", "term"), "doc", None),
        P(("dom", "term"), "doc", None),
        P(("dom", "term"), "doc"),
    )
    return jax.shard_map(
        functools.partial(local, mesh.shape["term"]),
        mesh=mesh,
        in_specs=placed,
        out_specs=(P(("dom", "term", "doc"), None), P(None, ("dom", "term", "doc"))),
        check_vma=False,
    )
```

```python
import functools

import jax
import jax.numpy as jnp
from jax import lax
from jax.experimental import pallas as pl
from jax.experimental.pallas import tpu as pltpu
from jax.sharding import PartitionSpec as P

MESH = pl.DeviceIdType.MESH
F32 = jnp.float32
BF16 = jnp.bfloat16
CHUNKS = 4
LOADS = 8
GROUP = 8
PIECES = 8
SCALE_ROWS = 16
NUMERATOR_SCALE = 65536.0


def dot(a, b):
    return jnp.dot(a, b, preferred_element_type=F32)


def dot_nt(a, b):
    return lax.dot_general(a, b, (((1,), (1,)), ((), ())), preferred_element_type=F32)


def two_parts(a):
    top = a.astype(BF16)
    return top, (a - top.astype(F32)).astype(BF16)


def power(v, squarings):
    size = v
    for _ in range(squarings):
        size = size * size
    return jnp.where(v < 0, -size, size).astype(BF16)


def root(code, squarings):
    code = code.astype(F32)
    size = jnp.abs(code)
    for _ in range(squarings):
        size = jnp.sqrt(size)
    return jnp.where(code < 0, -size, size)


def pack(ref, slot, value):
    rows = value.shape[0]
    top = jnp.max(jnp.abs(value), axis=0, keepdims=True)
    scale = jnp.maximum(top, 1e-30).astype(BF16).astype(F32)
    ref[slot, :rows] = power(value * (1.0 / scale), 3)
    ref[slot, rows:] = jnp.broadcast_to(scale, (SCALE_ROWS, value.shape[1])).astype(BF16)


def unpack(ref, slot, rows):
    scale = ref[slot, rows:].astype(F32)[:1]
    return root(ref[slot, :rows], 3) * scale


def norms(gram):
    k = gram.shape[0]
    row = lax.broadcasted_iota(jnp.int32, (k, k), 0)
    col = lax.broadcasted_iota(jnp.int32, (k, k), 1)
    square = jnp.sum(jnp.where(row == col, gram, 0.0), axis=1, keepdims=True)
    return jnp.maximum(jnp.sqrt(square), 1e-30) * NUMERATOR_SCALE


def link_slots(count, slots, rows, cols, out):
    span = rows.shape[1]
    slot = lax.broadcasted_iota(jnp.int32, (span, span), 0)
    at = lax.broadcasted_iota(jnp.int32, (span, span), 1)
    live = slot < count

    def latest(keys, wanted, limit):
        down = jnp.max(jnp.where(slot == at, keys, -1), axis=1, keepdims=True)
        hit = (down == wanted) & (slot < limit) & live
        found = jnp.max(jnp.where(hit, slot, -1), axis=0, keepdims=True)
        return jnp.where(found < 0, slots, found)

    out[0:1, :span] = latest(cols, cols, at)
    out[1:2, :span] = latest(rows, rows, at)
    out[2:3, :span] = rows
    out[3:4, :span] = cols
    out[4:5, :span] = latest(cols, at, slots)
    out[5:6, :span] = latest(rows, at, slots)


def kernel(
    n, slots, own, width,
    count, rows_ref, cols_ref, w_ref, h_hbm, x_hbm,
    w_out, h_out,
    links_v, links, links_sem, x, h_in, wt, prod, back, num_out, num_in, h_all, gw, gw_in, gw_parts,
    gh, gh_in, gh_pair, gh_all, gh_full, y_out, y_in, z_out, z_in,
    load_sem, hin_sem, wsend, wpass, wrecv, gwsem, nsend, nrecv, hsend, hrecv, hout_sem,
    ghsem, gasend, garecv, ysend, yrecv, zsend, zrecv,
):
    me = lax.axis_index("term")
    doc = lax.axis_index("doc")
    other = 1 - doc
    pairs = n // 2
    side, place = lax.rem(me, 2), lax.div(me, 2)
    mate = me + 1 - 2 * side
    k = w_ref.shape[1]
    per = own // CHUNKS
    load_size = slots // LOADS
    half = k // 2

    def load(i):
        part = pl.ds(i * load_size, load_size)
        return pltpu.make_async_copy(x_hbm.at[part], x.at[part], load_sem.at[i])

    def line(o):
        return lax.rem(place + o, pairs)

    def to_term(src, dst, send, recv, target):
        return pltpu.make_async_remote_copy(
            src_ref=src, dst_ref=dst, send_sem=send, recv_sem=recv,
            device_id={"term": target}, device_id_type=MESH,
        )

    def to_core(src, dst, send, recv):
        return pltpu.make_async_remote_copy(
            src_ref=src, dst_ref=dst, send_sem=send, recv_sem=recv,
            device_id={"doc": other}, device_id_type=MESH,
        )

    barrier = pltpu.get_barrier_semaphore()
    pl.semaphore_signal(barrier, inc=1, device_id={"doc": other}, device_id_type=MESH)
    pl.semaphore_signal(barrier, inc=1, device_id={"term": mate}, device_id_type=MESH)

    def greet(o, _):
        pl.semaphore_signal(barrier, inc=1, device_id={"term": 2 * line(o) + side}, device_id_type=MESH)
        return 0

    lax.fori_loop(1, pairs, greet, 0)
    for i in range(LOADS):
        load(i).start()
    h_load = pltpu.make_async_copy(h_hbm, h_in, hin_sem)
    h_load.start()
    wt[me] = w_ref[...].astype(F32).T.astype(BF16)
    link_slots(count[0, 0], slots, rows_ref[...], cols_ref[...], links_v)
    links_copy = pltpu.make_async_copy(links_v, links, links_sem)
    links_copy.start()
    pl.semaphore_wait(barrier, pairs + 1)

    def w_copy(slot, at):
        return to_term(wt.at[slot], wt.at[slot], wsend.at[at], wrecv.at[slot], 2 * at + side)

    def w_pass(slot):
        return to_term(wt.at[slot], wt.at[slot], wpass.at[lax.div(slot, 2)], wrecv.at[slot], mate)

    def send_w(o, _):
        w_copy(me, line(o)).start()
        return 0

    lax.fori_loop(1, pairs, send_w, 0)
    w_pass(me).start()
    prod[slots] = jnp.zeros_like(prod[slots])
    back[slots] = jnp.zeros_like(back[slots])
    gw[...] = dot_nt(wt[me], wt[me])

    def take_w(o, _):
        at = line(pairs - o)
        source = 2 * at + side
        w_copy(source, at).wait_recv()
        w_pass(source).start()
        gw[...] += dot_nt(wt[source], wt[source])
        return 0

    lax.fori_loop(1, pairs, take_w, 0)

    def take_passed(o, _):
        source = 2 * line(pairs - o) + 1 - side
        w_pass(source).wait_recv()
        gw[...] += dot_nt(wt[source], wt[source])
        return 0

    lax.fori_loop(0, pairs, take_passed, 0)
    links_copy.wait()
    gw_copy = to_core(gw, gw_in, gwsem.at[0], gwsem.at[1])
    gw_copy.start()

    for i in range(LOADS):
        load(i).wait()

        def forward(g, _):
            ids = [g * GROUP + t for t in range(GROUP)]
            terms = [dot(wt[links[2, s]], x[s]) for s in ids]
            for s, term in zip(ids, terms):
                prod[s] = prod[links[0, s]] + term
            return 0

        lax.fori_loop(i * load_size // GROUP, (i + 1) * load_size // GROUP, forward, 0)

    def num_copy(i):
        part = pl.ds(i * per, per)
        return to_core(num_out.at[part], num_in.at[part], nsend.at[i], nrecv.at[i])

    inverse = 1.0 / norms(gw[...])
    for i in range(CHUNKS):

        def stage(j, _):
            num_out[j] = power(prod[links[4, other * own + j]] * inverse, 2)
            return 0

        lax.fori_loop(i * per, (i + 1) * per, stage, 0)
        num_copy(i).start()

    gw_copy.wait()
    top, low = two_parts(gw[...] + gw_in[...])
    gw_parts[:, :k] = top
    gw_parts[:, k:] = low
    sent_scale = norms(gw_in[...])
    gh[...] = jnp.zeros_like(gh)
    h_load.wait()

    def h_copy(i):
        part = pl.ds(doc * own + i * per, per)
        return to_core(h_all.at[part], h_all.at[part], hsend.at[i], hrecv.at[i])

    def h_take(i):
        part = pl.ds(other * own + i * per, per)
        return to_core(h_all.at[part], h_all.at[part], hsend.at[i], hrecv.at[i])

    def h_store(j):
        cols = pl.ds(pl.multiple_of(j * width, width), width)
        return pltpu.make_async_copy(h_all.at[doc * own + j], h_out.at[:, cols], hout_sem.at[j])

    for i in range(CHUNKS):
        num_copy(i).wait()

        def update(g, _):
            news = []
            for j in (2 * g, 2 * g + 1):
                cols = pl.ds(pl.multiple_of(j * width, width), width)
                old = h_in[:, cols]
                denominator = dot(gw_parts[...], jnp.concatenate([old, old], axis=0))
                numerator = prod[links[4, doc * own + j]] + root(num_in[j], 2) * sent_scale
                new = (old.astype(F32) * numerator / denominator).astype(BF16)
                h_all[doc * own + j] = new
                news.append(new)
            gh[...] += dot_nt(news[0], news[0]) + dot_nt(news[1], news[1])
            for j in (2 * g, 2 * g + 1):
                h_store(j).start()
            return 0

        lax.fori_loop(i * per // 2, (i + 1) * per // 2, update, 0)
        h_copy(i).start()

    my_half = pl.ds(pl.multiple_of(doc * half, half), half)
    its_half = pl.ds(pl.multiple_of(other * half, half), half)
    gh_copy = to_core(gh.at[its_half], gh_in, ghsem.at[0], ghsem.at[1])
    gh_copy.start()
    gh_copy.wait()
    gh_pair[0] = gh[my_half] + gh_in[...]
    pair_copy = to_term(gh_pair.at[0], gh_pair.at[1], ghsem.at[2], ghsem.at[3], mate)
    pair_copy.start()
    for i in range(CHUNKS):
        h_take(i).wait_recv()
    pair_copy.wait()
    gh_all[place] = gh_pair[0] + gh_pair[1]

    def ga_copy(slot, at):
        return to_term(gh_all.at[slot], gh_all.at[slot], gasend.at[at], garecv.at[slot], 2 * at + side)

    def send_ga(o, _):
        ga_copy(place, line(o)).start()
        return 0

    lax.fori_loop(1, pairs, send_ga, 0)

    def backward(g, _):
        ids = [g * GROUP + t for t in range(GROUP)]
        terms = [dot_nt(x[s], h_all[links[3, s]]) for s in ids]
        for s, term in zip(ids, terms):
            back[s] = back[links[1, s]] + term
        return 0

    lax.fori_loop(0, slots // GROUP, backward, 0)

    def y_copy(at):
        return to_term(y_out.at[at], y_in.at[at], ysend.at[at], yrecv.at[at], mate)

    def z_copy(at):
        return to_term(z_out.at[at], z_in.at[place], zsend.at[at], zrecv.at[place], 2 * at + side)

    def z_take(at):
        return to_term(z_out.at[at], z_in.at[at], zsend.at[at], zrecv.at[at], 2 * at + side)

    def send_mate(o, _):
        at = line(o)
        pack(y_out, at, back[links[5, 2 * at + 1 - side]])
        y_copy(at).start()
        return 0

    lax.fori_loop(1, pairs + 1, send_mate, 0)

    def send_line(o, _):
        at = line(o)
        y_copy(at).wait_recv()
        pack(z_out, at, back[links[5, 2 * at + side]] + unpack(y_in, at, width))
        z_copy(at).start()
        return 0

    lax.fori_loop(1, pairs, send_line, 0)

    def take_ga(o, total):
        at = line(pairs - o)
        ga_copy(at, at).wait_recv()
        return total + gh_all[at]

    gh_full[my_half] = lax.fori_loop(1, pairs, take_ga, gh_all[place])
    full_copy = to_core(gh_full.at[my_half], gh_full.at[my_half], ghsem.at[4], ghsem.at[5])
    full_copy.start()
    y_copy(place).wait_recv()
    mine = back[links[5, me]] + unpack(y_in, place, width)
    full_take = to_core(gh_full.at[its_half], gh_full.at[its_half], ghsem.at[4], ghsem.at[5])
    full_take.wait_recv()
    top, low = two_parts(gh_full[...])
    w = w_ref[...]
    denominator = dot(w, top) + dot(w, low)

    def take_line(o, total):
        at = line(pairs - o)
        z_take(at).wait_recv()
        return total + unpack(z_in, at, width)

    numerator = lax.fori_loop(1, pairs, take_line, mine)
    w_out[...] = (w.astype(F32) * numerator / denominator).astype(BF16)

    def settle(o, _):
        at = line(o)
        w_copy(me, at).wait_send()
        ga_copy(place, at).wait_send()
        z_copy(at).wait_send()
        return 0

    lax.fori_loop(1, pairs, settle, 0)

    def settle_mate(at, _):
        w_pass(2 * at + side).wait_send()
        y_copy(at).wait_send()
        return 0

    lax.fori_loop(0, pairs, settle_mate, 0)
    full_copy.wait_send()
    for i in range(CHUNKS):
        h_copy(i).wait_send()

    def stored(j, _):
        h_store(j).wait()
        return 0

    lax.fori_loop(0, own, stored, 0)


def hand_over(w_ref, h_ref, w_out, h_out, w, h, sem):
    rows = h.shape[0] // PIECES
    ways = [(w_ref, w, w_out)]
    for i in range(PIECES):
        part = pl.ds(i * rows, rows)
        ways.append((h_ref.at[part], h.at[part], h_out.at[part]))
    into = [pltpu.make_async_copy(a, b, sem.at[0, i]) for i, (a, b, _) in enumerate(ways)]
    away = [pltpu.make_async_copy(b, c, sem.at[1, i]) for i, (_, b, c) in enumerate(ways)]
    for copy in into:
        copy.start()
    for first, second in zip(into, away):
        first.wait()
        second.start()
    for copy in away:
        copy.wait()


def local(n, w_rows, h_cols, blocks, block_row, block_col, block_count):
    k = w_rows.shape[1]
    slots, width = blocks.shape[2], blocks.shape[3]
    own_cols = h_cols.shape[1]
    own = own_cols // width
    grid_cols = 2 * own
    span = max(slots, grid_cols, n)
    wide = lambda a: jnp.pad(a[0], ((0, 0), (0, span - slots)))
    dma = pltpu.SemaphoreType.DMA
    w_next, h_next = pl.pallas_call(
        functools.partial(kernel, n, slots, own, width),
        out_shape=(
            jax.ShapeDtypeStruct(w_rows.shape, BF16),
            jax.ShapeDtypeStruct(h_cols.shape, BF16),
        ),
        in_specs=[
            pl.BlockSpec(memory_space=pltpu.SMEM),
            pl.BlockSpec(memory_space=pltpu.VMEM),
            pl.BlockSpec(memory_space=pltpu.VMEM),
            pl.BlockSpec(memory_space=pltpu.VMEM),
            pl.BlockSpec(memory_space=pl.ANY),
            pl.BlockSpec(memory_space=pl.ANY),
        ],
        out_specs=(pl.BlockSpec(memory_space=pltpu.VMEM), pl.BlockSpec(memory_space=pl.ANY)),
        scratch_shapes=[
            pltpu.VMEM((8, max(span, 128)), jnp.int32),
            pltpu.SMEM((8, max(span, 128)), jnp.int32),
            dma,
            pltpu.VMEM((slots, width, width), BF16),
            pltpu.VMEM((k, own_cols), BF16),
            pltpu.VMEM((n, k, width), BF16),
            pltpu.VMEM((slots + 1, k, width), F32),
            pltpu.VMEM((slots + 1, width, k), F32),
            pltpu.VMEM((own, k, width), BF16),
            pltpu.VMEM((own, k, width), BF16),
            pltpu.VMEM((grid_cols, k, width), BF16),
            pltpu.VMEM((k, k), F32),
            pltpu.VMEM((k, k), F32),
            pltpu.VMEM((k, 2 * k), BF16),
            pltpu.VMEM((k, k), F32),
            pltpu.VMEM((k // 2, k), F32),
            pltpu.VMEM((2, k // 2, k), F32),
            pltpu.VMEM((n // 2, k // 2, k), F32),
            pltpu.VMEM((k, k), F32),
            pltpu.VMEM((n // 2, width + SCALE_ROWS, k), BF16),
            pltpu.VMEM((n // 2, width + SCALE_ROWS, k), BF16),
            pltpu.VMEM((n // 2, width + SCALE_ROWS, k), BF16),
            pltpu.VMEM((n // 2, width + SCALE_ROWS, k), BF16),
            dma((LOADS,)),
            dma,
            dma((n // 2,)),
            dma((n // 2,)),
            dma((n,)),
            dma((2,)),
            dma((CHUNKS,)),
            dma((CHUNKS,)),
            dma((CHUNKS,)),
            dma((CHUNKS,)),
            dma((own,)),
            dma((6,)),
            dma((n // 2,)),
            dma((n // 2,)),
            dma((n // 2,)),
            dma((n // 2,)),
            dma((n // 2,)),
            dma((n // 2,)),
        ],
        compiler_params=pltpu.CompilerParams(
            collective_id=0, has_side_effects=True, vmem_limit_bytes=58 * 1024 * 1024
        ),
        cost_estimate=pl.CostEstimate(flops=4 * slots * width * width * k, bytes_accessed=2 * slots * width * width, transcendentals=0),
    )(block_count, wide(block_row), wide(block_col), w_rows, h_cols, blocks[0, 0])
    return pl.pallas_call(
        hand_over,
        out_shape=(
            jax.ShapeDtypeStruct(w_rows.shape, BF16),
            jax.ShapeDtypeStruct(h_cols.shape, BF16),
        ),
        in_specs=[pl.BlockSpec(memory_space=pl.ANY)] * 2,
        out_specs=(pl.BlockSpec(memory_space=pl.ANY),) * 2,
        scratch_shapes=[
            pltpu.VMEM(w_rows.shape, BF16),
            pltpu.VMEM(h_cols.shape, BF16),
            dma((2, PIECES + 1)),
        ],
    )(w_next, h_next)


def solution(mesh):
    placed = (
        P(("dom", "term", "doc"), None),
        P(None, ("dom", "term", "doc")),
        P(("dom", "term"), "doc", None, None, None),
        P(("dom", "term"), "doc", None),
        P(("dom", "term"), "doc", None),
        P(("dom", "term"), "doc"),
    )
    return jax.shard_map(
        functools.partial(local, mesh.shape["term"]),
        mesh=mesh,
        in_specs=placed,
        out_specs=(P(("dom", "term", "doc"), None), P(None, ("dom", "term", "doc"))),
        check_vma=False,
    )
```

```python
import functools

import jax
import jax.numpy as jnp
from jax import lax
from jax.experimental import pallas as pl
from jax.experimental.pallas import tpu as pltpu
from jax.sharding import PartitionSpec as P

MESH = pl.DeviceIdType.MESH
F32 = jnp.float32
BF16 = jnp.bfloat16
CHUNKS = 4
LOADS = 8
GROUP = 8
UPDATES = 4
PIECES = 8
SCALE_ROWS = 16
NUMERATOR_SCALE = 65536.0


def dot(a, b):
    return jnp.dot(a, b, preferred_element_type=F32)


def dot_nt(a, b):
    return lax.dot_general(a, b, (((1,), (1,)), ((), ())), preferred_element_type=F32)


def two_parts(a):
    top = a.astype(BF16)
    return top, (a - top.astype(F32)).astype(BF16)


def power(v, squarings):
    size = v
    for _ in range(squarings):
        size = size * size
    return jnp.where(v < 0, -size, size).astype(BF16)


def root(code, squarings):
    code = code.astype(F32)
    size = jnp.abs(code)
    for _ in range(squarings):
        size = jnp.sqrt(size)
    return jnp.where(code < 0, -size, size)


def pack(ref, slot, value):
    rows = value.shape[0]
    top = jnp.max(jnp.abs(value), axis=0, keepdims=True)
    scale = jnp.maximum(top, 1e-30).astype(BF16).astype(F32)
    ref[slot, :rows] = power(value * (1.0 / scale), 3)
    ref[slot, rows:] = jnp.broadcast_to(scale, (SCALE_ROWS, value.shape[1])).astype(BF16)


def unpack(ref, slot, rows):
    scale = ref[slot, rows:].astype(F32)[:1]
    return root(ref[slot, :rows], 3) * scale


def norms(gram):
    k = gram.shape[0]
    row = lax.broadcasted_iota(jnp.int32, (k, k), 0)
    col = lax.broadcasted_iota(jnp.int32, (k, k), 1)
    square = jnp.sum(jnp.where(row == col, gram, 0.0), axis=1, keepdims=True)
    return jnp.maximum(jnp.sqrt(square), 1e-30) * NUMERATOR_SCALE


def link_slots(count, slots, rows, cols, out):
    span = rows.shape[1]
    slot = lax.broadcasted_iota(jnp.int32, (span, span), 0)
    at = lax.broadcasted_iota(jnp.int32, (span, span), 1)
    live = slot < count

    def latest(keys, wanted, limit):
        down = jnp.max(jnp.where(slot == at, keys, -1), axis=1, keepdims=True)
        hit = (down == wanted) & (slot < limit) & live
        found = jnp.max(jnp.where(hit, slot, -1), axis=0, keepdims=True)
        return jnp.where(found < 0, slots, found)

    out[0:1, :span] = latest(cols, cols, at)
    out[1:2, :span] = latest(rows, rows, at)
    out[2:3, :span] = rows
    out[3:4, :span] = cols
    out[4:5, :span] = latest(cols, at, slots)
    out[5:6, :span] = latest(rows, at, slots)


def kernel(
    n, slots, own, width,
    count, rows_ref, cols_ref, w_ref, h_hbm, x_hbm,
    w_out, h_out,
    links_v, links, links_sem, x, h_in, wt, prod, back, num_out, num_in, h_all, gw, gw_in, gw_parts,
    gh, gh_in, gh_pair, gh_all, gh_full, y_out, y_in, z_out, z_in,
    load_sem, hin_sem, wsend, wpass, wrecv, gwsem, nsend, nrecv, hsend, hrecv, hout_sem,
    ghsem, gasend, garecv, ysend, yrecv, zsend, zrecv,
):
    me = lax.axis_index("term")
    doc = lax.axis_index("doc")
    other = 1 - doc
    pairs = n // 2
    side, place = lax.rem(me, 2), lax.div(me, 2)
    mate = me + 1 - 2 * side
    k = w_ref.shape[1]
    per = own // CHUNKS
    load_size = slots // LOADS
    half = k // 2

    def load(i):
        part = pl.ds(i * load_size, load_size)
        return pltpu.make_async_copy(x_hbm.at[part], x.at[part], load_sem.at[i])

    def line(o):
        return lax.rem(place + o, pairs)

    def to_term(src, dst, send, recv, target):
        return pltpu.make_async_remote_copy(
            src_ref=src, dst_ref=dst, send_sem=send, recv_sem=recv,
            device_id={"term": target}, device_id_type=MESH,
        )

    def to_core(src, dst, send, recv):
        return pltpu.make_async_remote_copy(
            src_ref=src, dst_ref=dst, send_sem=send, recv_sem=recv,
            device_id={"doc": other}, device_id_type=MESH,
        )

    barrier = pltpu.get_barrier_semaphore()
    pl.semaphore_signal(barrier, inc=1, device_id={"doc": other}, device_id_type=MESH)
    pl.semaphore_signal(barrier, inc=1, device_id={"term": mate}, device_id_type=MESH)

    def greet(o, _):
        pl.semaphore_signal(barrier, inc=1, device_id={"term": 2 * line(o) + side}, device_id_type=MESH)
        return 0

    lax.fori_loop(1, pairs, greet, 0)
    for i in range(LOADS):
        load(i).start()
    h_load = pltpu.make_async_copy(h_hbm, h_in, hin_sem)
    h_load.start()
    wt[me] = w_ref[...].astype(F32).T.astype(BF16)
    link_slots(count[0, 0], slots, rows_ref[...], cols_ref[...], links_v)
    links_copy = pltpu.make_async_copy(links_v, links, links_sem)
    links_copy.start()
    pl.semaphore_wait(barrier, pairs + 1)

    def w_hop(at, way):
        slot = 2 * at + side
        step = 1 if way else -1
        return to_term(wt.at[slot], wt.at[slot], wsend.at[way, at], wrecv.at[slot], me + 2 * step)

    def w_hops(at, act):
        @pl.when((at <= place) & (place < pairs - 1))
        def _():
            act(w_hop(at, 1))

        @pl.when((at >= place) & (place > 0))
        def _():
            act(w_hop(at, 0))

    def w_pass(slot):
        return to_term(wt.at[slot], wt.at[slot], wpass.at[lax.div(slot, 2)], wrecv.at[slot], mate)

    w_hops(place, lambda copy: copy.start())
    w_pass(me).start()
    prod[slots] = jnp.zeros_like(prod[slots])
    back[slots] = jnp.zeros_like(back[slots])
    gw[...] = dot_nt(wt[me], wt[me])

    def take_w(o, _):
        def take(at):
            source = 2 * at + side
            w_hop(at, 0).wait_recv()
            w_hops(at, lambda copy: copy.start())
            w_pass(source).start()
            gw[...] += dot_nt(wt[source], wt[source])

        @pl.when(place >= o)
        def _():
            take(place - o)

        @pl.when(place + o < pairs)
        def _():
            take(place + o)

        return 0

    lax.fori_loop(1, pairs, take_w, 0)

    def take_passed(o, _):
        source = 2 * line(pairs - o) + 1 - side
        w_pass(source).wait_recv()
        gw[...] += dot_nt(wt[source], wt[source])
        return 0

    lax.fori_loop(0, pairs, take_passed, 0)
    links_copy.wait()
    gw_copy = to_core(gw, gw_in, gwsem.at[0], gwsem.at[1])
    gw_copy.start()

    for i in range(LOADS):
        load(i).wait()

        def forward(g, _):
            ids = [g * GROUP + t for t in range(GROUP)]
            terms = [dot(wt[links[2, s]], x[s]) for s in ids]
            for s, term in zip(ids, terms):
                prod[s] = prod[links[0, s]] + term
            return 0

        lax.fori_loop(i * load_size // GROUP, (i + 1) * load_size // GROUP, forward, 0)

    def num_copy(i):
        part = pl.ds(i * per, per)
        return to_core(num_out.at[part], num_in.at[part], nsend.at[i], nrecv.at[i])

    inverse = 1.0 / norms(gw[...])
    for i in range(CHUNKS):

        def stage(j, _):
            num_out[j] = power(prod[links[4, other * own + j]] * inverse, 2)
            return 0

        lax.fori_loop(i * per, (i + 1) * per, stage, 0)
        num_copy(i).start()

    gw_copy.wait()
    top, low = two_parts(gw[...] + gw_in[...])
    gw_parts[:, :k] = top
    gw_parts[:, k:] = low
    sent_scale = norms(gw_in[...])
    gh[...] = jnp.zeros_like(gh)
    h_load.wait()

    def h_copy(i):
        part = pl.ds(doc * own + i * per, per)
        return to_core(h_all.at[part], h_all.at[part], hsend.at[i], hrecv.at[i])

    def h_take(i):
        part = pl.ds(other * own + i * per, per)
        return to_core(h_all.at[part], h_all.at[part], hsend.at[i], hrecv.at[i])

    def h_store(j):
        cols = pl.ds(pl.multiple_of(j * width, width), width)
        return pltpu.make_async_copy(h_all.at[doc * own + j], h_out.at[:, cols], hout_sem.at[j])

    for i in range(CHUNKS):
        num_copy(i).wait()

        def update(g, _):
            news = []
            for j in [UPDATES * g + t for t in range(UPDATES)]:
                cols = pl.ds(pl.multiple_of(j * width, width), width)
                old = h_in[:, cols]
                denominator = dot(gw_parts[...], jnp.concatenate([old, old], axis=0))
                numerator = prod[links[4, doc * own + j]] + root(num_in[j], 2) * sent_scale
                new = (old.astype(F32) * numerator / denominator).astype(BF16)
                h_all[doc * own + j] = new
                news.append(new)
            gh[...] += sum(dot_nt(new, new) for new in news)
            for t in range(UPDATES):
                h_store(UPDATES * g + t).start()
            return 0

        lax.fori_loop(i * per // UPDATES, (i + 1) * per // UPDATES, update, 0)
        h_copy(i).start()

    my_half = pl.ds(pl.multiple_of(doc * half, half), half)
    its_half = pl.ds(pl.multiple_of(other * half, half), half)
    gh_copy = to_core(gh.at[its_half], gh_in, ghsem.at[0], ghsem.at[1])
    gh_copy.start()
    gh_copy.wait()
    gh_pair[0] = gh[my_half] + gh_in[...]
    pair_copy = to_term(gh_pair.at[0], gh_pair.at[1], ghsem.at[2], ghsem.at[3], mate)
    pair_copy.start()
    for i in range(CHUNKS):
        h_take(i).wait_recv()
    pair_copy.wait()
    gh_all[place] = gh_pair[0] + gh_pair[1]

    def ga_copy(slot, at):
        return to_term(gh_all.at[slot], gh_all.at[slot], gasend.at[at], garecv.at[slot], 2 * at + side)

    def send_ga(o, _):
        ga_copy(place, line(o)).start()
        return 0

    lax.fori_loop(1, pairs, send_ga, 0)

    def backward(g, _):
        ids = [g * GROUP + t for t in range(GROUP)]
        terms = [dot_nt(x[s], h_all[links[3, s]]) for s in ids]
        for s, term in zip(ids, terms):
            back[s] = back[links[1, s]] + term
        return 0

    lax.fori_loop(0, slots // GROUP, backward, 0)

    def y_copy(at):
        return to_term(y_out.at[at], y_in.at[at], ysend.at[at], yrecv.at[at], mate)

    def z_copy(at):
        return to_term(z_out.at[at], z_in.at[place], zsend.at[at], zrecv.at[place], 2 * at + side)

    def z_take(at):
        return to_term(z_out.at[at], z_in.at[at], zsend.at[at], zrecv.at[at], 2 * at + side)

    def send_mate(o, _):
        at = line(o)
        pack(y_out, at, back[links[5, 2 * at + 1 - side]])
        y_copy(at).start()
        return 0

    lax.fori_loop(1, pairs + 1, send_mate, 0)

    def send_line(o, _):
        at = line(o)
        y_copy(at).wait_recv()
        pack(z_out, at, back[links[5, 2 * at + side]] + unpack(y_in, at, width))
        z_copy(at).start()
        return 0

    lax.fori_loop(1, pairs, send_line, 0)

    def take_ga(o, total):
        at = line(pairs - o)
        ga_copy(at, at).wait_recv()
        return total + gh_all[at]

    gh_full[my_half] = lax.fori_loop(1, pairs, take_ga, gh_all[place])
    full_copy = to_core(gh_full.at[my_half], gh_full.at[my_half], ghsem.at[4], ghsem.at[5])
    full_copy.start()
    y_copy(place).wait_recv()
    mine = back[links[5, me]] + unpack(y_in, place, width)
    full_take = to_core(gh_full.at[its_half], gh_full.at[its_half], ghsem.at[4], ghsem.at[5])
    full_take.wait_recv()
    top, low = two_parts(gh_full[...])
    w = w_ref[...]
    denominator = dot(w, top) + dot(w, low)

    def take_line(o, total):
        at = line(pairs - o)
        z_take(at).wait_recv()
        return total + unpack(z_in, at, width)

    numerator = lax.fori_loop(1, pairs, take_line, mine)
    w_out[...] = (w.astype(F32) * numerator / denominator).astype(BF16)

    def settle(o, _):
        at = line(o)
        ga_copy(place, at).wait_send()
        z_copy(at).wait_send()
        return 0

    lax.fori_loop(1, pairs, settle, 0)

    def settle_mate(at, _):
        w_hops(at, lambda copy: copy.wait_send())
        w_pass(2 * at + side).wait_send()
        y_copy(at).wait_send()
        return 0

    lax.fori_loop(0, pairs, settle_mate, 0)
    full_copy.wait_send()
    for i in range(CHUNKS):
        h_copy(i).wait_send()

    def stored(j, _):
        h_store(j).wait()
        return 0

    lax.fori_loop(0, own, stored, 0)


def hand_over(w_ref, h_ref, w_out, h_out, w, h, sem):
    rows = h.shape[0] // PIECES
    ways = [(w_ref, w, w_out)]
    for i in range(PIECES):
        part = pl.ds(i * rows, rows)
        ways.append((h_ref.at[part], h.at[part], h_out.at[part]))
    into = [pltpu.make_async_copy(a, b, sem.at[0, i]) for i, (a, b, _) in enumerate(ways)]
    away = [pltpu.make_async_copy(b, c, sem.at[1, i]) for i, (_, b, c) in enumerate(ways)]
    for copy in into:
        copy.start()
    for first, second in zip(into, away):
        first.wait()
        second.start()
    for copy in away:
        copy.wait()


def local(n, w_rows, h_cols, blocks, block_row, block_col, block_count):
    k = w_rows.shape[1]
    slots, width = blocks.shape[2], blocks.shape[3]
    own_cols = h_cols.shape[1]
    own = own_cols // width
    grid_cols = 2 * own
    span = max(slots, grid_cols, n)
    wide = lambda a: jnp.pad(a[0], ((0, 0), (0, span - slots)))
    dma = pltpu.SemaphoreType.DMA
    w_next, h_next = pl.pallas_call(
        functools.partial(kernel, n, slots, own, width),
        out_shape=(
            jax.ShapeDtypeStruct(w_rows.shape, BF16),
            jax.ShapeDtypeStruct(h_cols.shape, BF16),
        ),
        in_specs=[
            pl.BlockSpec(memory_space=pltpu.SMEM),
            pl.BlockSpec(memory_space=pltpu.VMEM),
            pl.BlockSpec(memory_space=pltpu.VMEM),
            pl.BlockSpec(memory_space=pltpu.VMEM),
            pl.BlockSpec(memory_space=pl.ANY),
            pl.BlockSpec(memory_space=pl.ANY),
        ],
        out_specs=(pl.BlockSpec(memory_space=pltpu.VMEM), pl.BlockSpec(memory_space=pl.ANY)),
        scratch_shapes=[
            pltpu.VMEM((8, max(span, 128)), jnp.int32),
            pltpu.SMEM((8, max(span, 128)), jnp.int32),
            dma,
            pltpu.VMEM((slots, width, width), BF16),
            pltpu.VMEM((k, own_cols), BF16),
            pltpu.VMEM((n, k, width), BF16),
            pltpu.VMEM((slots + 1, k, width), F32),
            pltpu.VMEM((slots + 1, width, k), F32),
            pltpu.VMEM((own, k, width), BF16),
            pltpu.VMEM((own, k, width), BF16),
            pltpu.VMEM((grid_cols, k, width), BF16),
            pltpu.VMEM((k, k), F32),
            pltpu.VMEM((k, k), F32),
            pltpu.VMEM((k, 2 * k), BF16),
            pltpu.VMEM((k, k), F32),
            pltpu.VMEM((k // 2, k), F32),
            pltpu.VMEM((2, k // 2, k), F32),
            pltpu.VMEM((n // 2, k // 2, k), F32),
            pltpu.VMEM((k, k), F32),
            pltpu.VMEM((n // 2, width + SCALE_ROWS, k), BF16),
            pltpu.VMEM((n // 2, width + SCALE_ROWS, k), BF16),
            pltpu.VMEM((n // 2, width + SCALE_ROWS, k), BF16),
            pltpu.VMEM((n // 2, width + SCALE_ROWS, k), BF16),
            dma((LOADS,)),
            dma,
            dma((2, n // 2)),
            dma((n // 2,)),
            dma((n,)),
            dma((2,)),
            dma((CHUNKS,)),
            dma((CHUNKS,)),
            dma((CHUNKS,)),
            dma((CHUNKS,)),
            dma((own,)),
            dma((6,)),
            dma((n // 2,)),
            dma((n // 2,)),
            dma((n // 2,)),
            dma((n // 2,)),
            dma((n // 2,)),
            dma((n // 2,)),
        ],
        compiler_params=pltpu.CompilerParams(
            collective_id=0, has_side_effects=True, vmem_limit_bytes=58 * 1024 * 1024
        ),
        cost_estimate=pl.CostEstimate(flops=4 * slots * width * width * k, bytes_accessed=2 * slots * width * width, transcendentals=0),
    )(block_count, wide(block_row), wide(block_col), w_rows, h_cols, blocks[0, 0])
    return pl.pallas_call(
        hand_over,
        out_shape=(
            jax.ShapeDtypeStruct(w_rows.shape, BF16),
            jax.ShapeDtypeStruct(h_cols.shape, BF16),
        ),
        in_specs=[pl.BlockSpec(memory_space=pl.ANY)] * 2,
        out_specs=(pl.BlockSpec(memory_space=pl.ANY),) * 2,
        scratch_shapes=[
            pltpu.VMEM(w_rows.shape, BF16),
            pltpu.VMEM(h_cols.shape, BF16),
            dma((2, PIECES + 1)),
        ],
    )(w_next, h_next)


def solution(mesh):
    placed = (
        P(("dom", "term", "doc"), None),
        P(None, ("dom", "term", "doc")),
        P(("dom", "term"), "doc", None, None, None),
        P(("dom", "term"), "doc", None),
        P(("dom", "term"), "doc", None),
        P(("dom", "term"), "doc"),
    )
    return jax.shard_map(
        functools.partial(local, mesh.shape["term"]),
        mesh=mesh,
        in_specs=placed,
        out_specs=(P(("dom", "term", "doc"), None), P(None, ("dom", "term", "doc"))),
        check_vma=False,
    )
```
